32 devices in a mesh: row: 8 (over z, x), col: 4 (over y, core).
Axes of the slice: x: 2, y: 2, z: 4, core: 2. Of those that a mesh axis runs over, the one named last changes fastest.
Arguments:
- design_levels: int32 [32, 16384], P(None, ('row', 'col')), may hold values from 0 to 16383, each once within a row
- length_scales: float32 [32], replicated, may hold values from 1 to 3
- features: float32 [16384, 256], P(('row', 'col')), may hold values from -0.375 to 0.375
- noise: float32 [16384], P(('row', 'col')), may hold values from 0.25 to 2.5
- panel_index: int32 [1], replicated, may hold values from 0 to 31
Outputs:
- panel_factor: float32 [16384, 512], P('row')
- updated: float32 [16384, 16384], P('row', 'col')
The draws below stay inside these ranges and needn't reach their ends.
Inputs may be any that keep to these rules, and one draw needn't show every extreme that they name: Each row of design_levels is a permutation of 0 .. 16384 - 1 (a Latin hypercube).
All inputs are finite; a program needn't handle non-finite values.
Results may differ from the reference program's by a relative error of at most 0.0003.
Values sent between devices are 32-bit elements; how exact they have to be, the bound alone decides.
A program may use at most 192 MiB of HBM per device.

```python
import math
import jax
import jax.numpy as jnp
from jax import lax

N = 16384
INPUTS = 32
FEATS = 256
PANEL = 512


def block_scale(rng, extent, shards, smallest, largest):
    def one(position, blocks):
        draws = jax.random.uniform(jax.random.fold_in(jax.random.fold_in(rng, 6), position), (blocks,), jnp.float32, smallest / len(shards), largest / len(shards))
        return jnp.repeat(jnp.exp(draws), extent[position] // blocks).reshape((-1,) + (1,) * (len(extent) - position - 1))

    level = one(*shards[0])
    for cut in shards[1:]:
        level = level * one(*cut)
    return level


def centred(rng, dims, scale, limit, split=(), kind=jnp.bfloat16):
    values = jax.random.normal(rng, dims, jnp.float32) * scale
    if len(split) > 0:
        values = block_scale(rng, dims, split, -0.22, 0.18) * values
    return jnp.clip(values, min=-limit, max=limit).astype(kind)


def setup_inputs(seed: int = 0) -> dict:
    streams_of = jax.random.split(jax.random.key(seed), 6)
    return {
        "design_levels": jax.vmap(lambda own: jax.random.permutation(own, N))(jax.random.split(streams_of[0], INPUTS)).reshape((INPUTS, N)).astype(jnp.int32),
        "length_scales": jnp.clip(jnp.exp(jax.random.uniform(streams_of[1], (INPUTS,), jnp.float32, math.log(1.0), math.log(3.0))), 1.0, 3.0),
        "features": centred(streams_of[2], (N, FEATS), FEATS ** -0.5, 0.375, ((0, 32),), jnp.float32),
        "noise": jnp.clip(jnp.exp(math.log(2.5) - 2.3025851 * jax.random.uniform(streams_of[3], (N,), jnp.float32) ** block_scale(streams_of[3], (N,), ((0, 32),), -0.2, 0.2)), 0.25, 2.5),
        "panel_index": jax.random.randint(streams_of[4], (1,), 0, N // PANEL).astype(jnp.int32),
    }


def scale_points(levels, scales):
    return (levels.astype(jnp.float32) + 0.5) / N / scales[:, None]

def kernel_block(left_u, right_u, left_h, right_h, left_noise, left_start, right_start):
    left_sq = jnp.sum(left_u * left_u, axis=0)
    right_sq = jnp.sum(right_u * right_u, axis=0)
    cross = lax.dot_general(left_u.astype(jnp.float32), right_u.astype(jnp.float32), (((0,), (0,)), ((), ())), precision=lax.Precision.HIGHEST, preferred_element_type=jnp.float32)
    gram = lax.dot_general(left_h.astype(jnp.float32), right_h.astype(jnp.float32), (((1,), (1,)), ((), ())), precision=lax.Precision.HIGHEST, preferred_element_type=jnp.float32)
    left_ids = left_start + jnp.arange(left_u.shape[1], dtype=jnp.int32)
    right_ids = right_start + jnp.arange(right_u.shape[1], dtype=jnp.int32)
    same = left_ids[:, None] == right_ids[None, :]
    distance = left_sq[:, None] + right_sq[None, :] - 2.0 * cross
    return jnp.exp(-0.5 * distance) + gram + jnp.where(same, left_noise[:, None], jnp.zeros_like(gram))

def factor_inverse(block):
    lower = jnp.linalg.cholesky(block)
    identity = jnp.eye(block.shape[0], dtype=block.dtype)
    return lax.linalg.triangular_solve(lower, identity, left_side=True, lower=True)

def reference(design_levels, length_scales, features, noise, panel_index):
    scaled = scale_points(design_levels, length_scales)
    start = (panel_index[0] * PANEL).astype(jnp.int32)
    panel_u = lax.dynamic_slice_in_dim(scaled, start, PANEL, 1)
    panel_h = lax.dynamic_slice_in_dim(features, start, PANEL, 0)
    panel_noise = lax.dynamic_slice_in_dim(noise, start, PANEL, 0)
    inverse = factor_inverse(kernel_block(panel_u, panel_u, panel_h, panel_h, panel_noise, start, start))
    rows_blk = min(N, 1024)
    count = N // rows_blk

    def panel_rows(index):
        first = (index * rows_blk).astype(jnp.int32)
        block_u = lax.dynamic_slice_in_dim(scaled, first, rows_blk, 1)
        block_h = lax.dynamic_slice_in_dim(features, first, rows_blk, 0)
        block_noise = lax.dynamic_slice_in_dim(noise, first, rows_blk, 0)
        columns = kernel_block(block_u, panel_u, block_h, panel_h, block_noise, first, start)
        return jnp.dot(columns.astype(jnp.float32), inverse.T.astype(jnp.float32), precision=lax.Precision.HIGHEST, preferred_element_type=jnp.float32)
    panel_factor = lax.map(panel_rows, jnp.arange(count, dtype=jnp.int32)).reshape(N, PANEL)

    def update_rows(index):
        first = (index * rows_blk).astype(jnp.int32)
        block_u = lax.dynamic_slice_in_dim(scaled, first, rows_blk, 1)
        block_h = lax.dynamic_slice_in_dim(features, first, rows_blk, 0)
        block_noise = lax.dynamic_slice_in_dim(noise, first, rows_blk, 0)
        block_factor = lax.dynamic_slice_in_dim(panel_factor, first, rows_blk, 0)
        whole = kernel_block(block_u, scaled, block_h, features, block_noise, first, jnp.zeros((), jnp.int32))
        return whole - jnp.dot(block_factor.astype(jnp.float32), panel_factor.T.astype(jnp.float32), precision=lax.Precision.HIGHEST, preferred_element_type=jnp.float32)
    updated = lax.map(update_rows, jnp.arange(count, dtype=jnp.int32)).reshape(N, N)
    return (panel_factor, updated)
```

```python
import functools
import math

import jax
import jax.numpy as jnp
from jax import lax
from jax.experimental import pallas as pl
from jax.experimental.pallas import tpu as pltpu
from jax.sharding import PartitionSpec as P

BF = jnp.bfloat16
F32 = jnp.float32
LOG2E = math.log2(math.e)
BASE = 128
STRIP = 8
EXT = 40
EK = 256


def split2(x):
    hi = x.astype(BF)
    return hi, (x - hi.astype(F32)).astype(BF)


def split3(x):
    hi = x.astype(BF)
    rest = x - hi.astype(F32)
    mid = rest.astype(BF)
    return hi, mid, (rest - mid.astype(F32)).astype(BF)


def bdot(a, b):
    return jnp.dot(a, b, preferred_element_type=F32)


def dot3(a, b):
    (ah, al), (bh, bl) = a, b
    return bdot(ah, bh) + (bdot(ah, bl) + bdot(al, bh))


def fdot(a, b, dims):
    return lax.dot_general(
        a, b, (dims, ((), ())), precision=lax.Precision.HIGHEST, preferred_element_type=F32
    )


def exponent_operand(ext, inputs, left):
    width = ext.shape[1]
    root = math.sqrt(LOG2E)
    u = ext[:inputs] * root
    h, m, l = [part.astype(F32) for part in split3(u)]
    s = ext[inputs : inputs + 1] * (-0.5 * LOG2E)
    sh, sm, sl = [part.astype(F32) for part in split3(s)]
    row = lax.broadcasted_iota(jnp.int32, (8, width), 0)
    one = jnp.ones((8, width), F32)
    zero = jnp.zeros((8, width), F32)

    def norms(first):
        mine = jnp.where(
            row == first, sh, jnp.where(row == first + 1, sm, jnp.where(row == first + 2, sl, zero))
        )
        other = 3 - first
        ones = jnp.where((row >= other) & (row < other + 3), one, zero)
        return mine + ones

    if left:
        parts = [h, h, m, h, l, m, norms(0)]
    else:
        parts = [h, m, h, l, h, m, norms(3)]
    depth = 6 * inputs + 8
    parts.append(jnp.zeros((EK - depth, width), F32))
    return jnp.concatenate(parts, axis=0)


def factor_diagonal(d):
    n = d.shape[0]
    eye = (
        lax.broadcasted_iota(jnp.int32, (n, n), 0) == lax.broadcasted_iota(jnp.int32, (n, n), 1)
    ).astype(F32)
    rest_a = d
    rest_i = eye
    sub = lax.broadcasted_iota(jnp.int32, (STRIP, 1), 0)
    done = []
    for j in range(n // STRIP):
        strip = jnp.concatenate([rest_a[:STRIP], rest_i[:STRIP]], axis=1)
        first = j * STRIP
        cols = [
            jnp.broadcast_to(strip[:, first + i : first + i + 1], (STRIP, n)) for i in range(STRIP)
        ]
        for i in range(STRIP):
            inv = lax.rsqrt(cols[i][i : i + 1])
            col = cols[i] * inv
            row = strip[i : i + 1] * jnp.concatenate([inv, inv], axis=1)
            below = jnp.where(sub > i, col, 0.0)
            strip = jnp.where(sub == i, row, strip - jnp.concatenate([below, below], axis=1) * row)
            for k in range(i + 1, STRIP):
                cols[k] = cols[k] - below * col[k : k + 1]
        done.append(strip[:, n:])
        if j + 1 < n // STRIP:
            lead = strip[:, :n]
            change = fdot(lead, strip, ((0,), (0,)))[first + STRIP :]
            rest_a = rest_a[STRIP:] - change[:, :n]
            rest_i = rest_i[STRIP:] - change[:, n:]
    return jnp.concatenate(done, axis=0)


def inverse_kernel(inputs, feats, x_ref, hi_ref, lo_ref, t_ref):
    panel = x_ref.shape[1]
    h = x_ref[:feats, :]
    ext = x_ref[feats:, :]
    left = exponent_operand(ext, inputs, True).astype(BF)
    right = exponent_operand(ext, inputs, False).astype(BF)
    e = lax.dot_general(left, right, (((0,), (0,)), ((), ())), preferred_element_type=F32)
    gram = fdot(h, h, ((0,), (0,)))
    rows = lax.broadcasted_iota(jnp.int32, (panel, panel), 0)
    cols = lax.broadcasted_iota(jnp.int32, (panel, panel), 1)
    noise = ext[inputs + 1 : inputs + 2]
    t_ref[...] = jnp.exp2(e) + gram + jnp.where(rows == cols, noise, 0.0)
    count = panel // BASE
    for b in range(count):
        here = pl.ds(b * BASE, BASE)
        w = factor_diagonal(t_ref[here, here])
        r = fdot(w, t_ref[here, :], ((1,), (0,)))
        t_ref[here, :] = r
        t_ref[here, here] = w
        if b + 1 < count:
            below = pl.ds((b + 1) * BASE, panel - (b + 1) * BASE)
            t_ref[below, here] = jnp.zeros((panel - (b + 1) * BASE, BASE), F32)
            t_ref[below, :] = t_ref[below, :] - fdot(
                t_ref[here, below], t_ref[here, :], ((0,), (0,))
            )
    inverse = jnp.where(rows >= cols, t_ref[...], 0.0)
    hi, lo = split2(inverse)
    hi_ref[...] = hi
    lo_ref[...] = lo


def main_kernel(
    inputs,
    feats,
    n_row,
    n_col,
    bm,
    bn,
    where_ref,
    xr_ref,
    xc_ref,
    xp_ref,
    ihi_ref,
    ilo_ref,
    pf_ref,
    out_ref,
    ah,
    al,
    ea,
    bh,
    bl,
    eb,
    pt,
    ptl,
    pe,
    pel,
    ph,
    phl,
    it,
    itl,
    nr,
):
    step = pl.program_id(0)
    panel = xp_ref.shape[1]
    pts = xr_ref.shape[2]
    half = panel // 2
    row_start = where_ref[0]
    col_start = where_ref[1]
    panel_start = where_ref[2]

    @pl.when(step == 0)
    def _():
        hp = xp_ref[:feats, :]
        ext = xp_ref[feats:, :]
        hi, lo = split2(hp)
        ph[...] = hi
        phl[...] = lo
        hi, lo = split2(hp.T)
        pt[...] = hi
        ptl[...] = lo
        pe[...] = exponent_operand(ext, inputs, False).astype(BF)
        pel[...] = exponent_operand(ext, inputs, True).T.astype(BF)
        it[...] = ihi_ref[...].astype(F32).T.astype(BF)
        itl[...] = ilo_ref[...].astype(F32).T.astype(BF)

    @pl.when(step < n_row)
    def _():
        h = split2(xr_ref[0, :feats, :].T)
        ext = xr_ref[0, feats:, :]
        e = exponent_operand(ext, inputs, True).T.astype(BF)
        k = jnp.exp2(bdot(e, pe[...])) + dot3(h, (ph[...], phl[...]))
        first = row_start + step * pts
        rows = first + lax.broadcasted_iota(jnp.int32, (pts, panel), 0)
        cols = panel_start + lax.broadcasted_iota(jnp.int32, (pts, panel), 1)
        noise_col = ext[inputs : inputs + 8].T[:, 1:2]
        k = k + jnp.where(rows == cols, noise_col, 0.0)
        kh, kl = split2(k)
        p0 = dot3(
            (kh[:, :half], kl[:, :half]), (it[:half, :half], itl[:half, :half])
        )
        p1 = dot3((kh, kl), (it[:, half:], itl[:, half:]))
        p = jnp.concatenate([p0, p1], axis=1)
        pf_ref[...] = p
        phi, plo = split2(-p)
        here = pl.ds(pl.multiple_of(step * pts, pts), pts)
        ah[here, :feats] = h[0]
        al[here, :feats] = h[1]
        ah[here, feats:] = phi
        al[here, feats:] = plo
        ea[here, :] = e
        nr[here, :] = jnp.broadcast_to(noise_col, (pts, 128))

    @pl.when((step >= n_row) & (step < n_row + n_col))
    def _():
        at = step - n_row
        h = split2(xc_ref[0, :feats, :])
        ext = xc_ref[0, feats:, :]
        e = exponent_operand(ext, inputs, False).astype(BF)
        k = jnp.exp2(bdot(pel[...], e)) + dot3((pt[...], ptl[...]), h)
        first = col_start + at * pts
        rows = panel_start + lax.broadcasted_iota(jnp.int32, (panel, pts), 0)
        cols = first + lax.broadcasted_iota(jnp.int32, (panel, pts), 1)
        k = k + jnp.where(rows == cols, ext[inputs + 1 : inputs + 2], 0.0)
        kh, kl = split2(k)
        p0 = dot3(
            (ihi_ref[:half, :half], ilo_ref[:half, :half]), (kh[:half], kl[:half])
        )
        p1 = dot3((ihi_ref[half:, :], ilo_ref[half:, :]), (kh, kl))
        phi, plo = split2(jnp.concatenate([p0, p1], axis=0))
        here = pl.ds(pl.multiple_of(at * pts, pts), pts)
        bh[:feats, here] = h[0]
        bl[:feats, here] = h[1]
        bh[feats:, here] = phi
        bl[feats:, here] = plo
        eb[:, here] = e

    @pl.when(step >= n_row + n_col)
    def _():
        at = step - n_row - n_col
        per = eb.shape[1] // bn
        i = at // per
        j = at - i * per
        rs = pl.ds(pl.multiple_of(i * bm, bm), bm)
        cs = pl.ds(pl.multiple_of(j * bn, bn), bn)
        a = (ah[rs, :], al[rs, :])
        b = (bh[:, cs], bl[:, cs])
        out_ref[...] = jnp.exp2(bdot(ea[rs, :], eb[:, cs])) + dot3(a, b)
        r0 = row_start + i * bm
        c0 = col_start + j * bn

        @pl.when((r0 < c0 + bn) & (c0 < r0 + bm))
        def _():
            for q in range(bn // 128):
                rows = r0 + lax.broadcasted_iota(jnp.int32, (bm, 128), 0)
                cols = c0 + q * 128 + lax.broadcasted_iota(jnp.int32, (bm, 128), 1)
                part = pl.ds(q * 128, 128)
                out_ref[:, part] = out_ref[:, part] + jnp.where(rows == cols, nr[rs, :], 0.0)


def shards(n_total, panel, design_levels, length_scales, features, noise, panel_index):
    n_rows = lax.axis_size("row")
    n_cols = lax.axis_size("col")
    ratio = n_rows // n_cols
    row_pos = lax.axis_index("row")
    col_pos = lax.axis_index("col")
    inputs, pts = design_levels.shape
    feats = features.shape[1]
    depth = feats + EXT

    u = (design_levels.astype(F32) + 0.5) / n_total / length_scales[:, None]
    s = jnp.sum(u * u, axis=0, keepdims=True)
    pad = jnp.zeros((EXT - inputs - 2, pts), F32)
    piece = jnp.concatenate([features.T, u, s, noise[None, :], pad], axis=0)

    start = panel_index[0] * panel
    mine = (row_pos * n_cols + col_pos) * pts
    if pts == panel:
        part = jnp.where(mine == start, piece, 0.0)
    else:
        offset = mine - start
        inside = (offset >= 0) & (offset < panel)
        part = lax.dynamic_update_slice(
            jnp.zeros((depth, panel), F32),
            jnp.where(inside, piece, 0.0),
            (0, jnp.where(inside, offset, 0)),
        )
    xp = lax.psum(part, ("row", "col"))

    xr = lax.all_gather(piece, "col", axis=0)
    pairs = []
    for r in range(n_rows):
        for c in range(n_cols):
            to = ((r % ratio) * n_cols + c) * n_cols + r // ratio
            pairs.append((r * n_cols + c, to))
    moved = lax.ppermute(piece, ("row", "col"), pairs)
    xc = lax.all_gather(moved, "row", axis=0)

    ihi, ilo = pl.pallas_call(
        functools.partial(inverse_kernel, inputs, feats),
        out_shape=[jax.ShapeDtypeStruct((panel, panel), BF)] * 2,
        in_specs=[pl.BlockSpec(memory_space=pltpu.VMEM)],
        out_specs=[pl.BlockSpec(memory_space=pltpu.VMEM)] * 2,
        scratch_shapes=[pltpu.VMEM((panel, panel), F32)],
        compiler_params=pltpu.CompilerParams(vmem_limit_bytes=40 * 2**20),
        cost_estimate=pl.CostEstimate(
            flops=60 * 10**9, bytes_accessed=2**21, transcendentals=2**18
        ),
        name="panel_inverse",
    )(xp)

    rows = pts * n_cols
    cols = pts * n_rows
    bm = min(512, rows)
    bn = min(1024, cols)
    per = cols // bn
    tiles = (rows // bm) * per
    lead = n_cols + n_rows
    row_start = row_pos * rows
    col_start = col_pos * cols
    where = jnp.stack([row_start, col_start, start]).astype(jnp.int32)

    def row_map(g, w):
        return (jnp.minimum(g, n_cols - 1), 0, 0)

    def col_map(g, w):
        return (jnp.clip(g - n_cols, 0, n_rows - 1), 0, 0)

    def out_map(g, w):
        t = jnp.maximum(g - lead, 0)
        return (t // per, t % per)

    k_all = feats + panel
    factor_rows, updated = pl.pallas_call(
        functools.partial(main_kernel, inputs, feats, n_cols, n_rows, bm, bn),
        out_shape=[
            jax.ShapeDtypeStruct((rows, panel), F32),
            jax.ShapeDtypeStruct((rows, cols), F32),
        ],
        grid_spec=pltpu.PrefetchScalarGridSpec(
            num_scalar_prefetch=1,
            grid=(lead + tiles,),
            in_specs=[
                pl.BlockSpec((1, depth, pts), row_map),
                pl.BlockSpec((1, depth, pts), col_map),
                pl.BlockSpec((depth, panel), lambda g, w: (0, 0)),
                pl.BlockSpec((panel, panel), lambda g, w: (0, 0)),
                pl.BlockSpec((panel, panel), lambda g, w: (0, 0)),
            ],
            out_specs=[
                pl.BlockSpec((pts, panel), lambda g, w: (jnp.minimum(g, n_cols - 1), 0)),
                pl.BlockSpec((bm, bn), out_map),
            ],
            scratch_shapes=[
                pltpu.VMEM((rows, k_all), BF),
                pltpu.VMEM((rows, k_all), BF),
                pltpu.VMEM((rows, EK), BF),
                pltpu.VMEM((k_all, cols), BF),
                pltpu.VMEM((k_all, cols), BF),
                pltpu.VMEM((EK, cols), BF),
                pltpu.VMEM((panel, feats), BF),
                pltpu.VMEM((panel, feats), BF),
                pltpu.VMEM((EK, panel), BF),
                pltpu.VMEM((panel, EK), BF),
                pltpu.VMEM((feats, panel), BF),
                pltpu.VMEM((feats, panel), BF),
                pltpu.VMEM((panel, panel), BF),
                pltpu.VMEM((panel, panel), BF),
                pltpu.VMEM((rows, 128), F32),
            ],
        ),
        compiler_params=pltpu.CompilerParams(
            dimension_semantics=("arbitrary",), vmem_limit_bytes=56 * 2**20
        ),
        cost_estimate=pl.CostEstimate(
            flops=2 * rows * cols * k_all * 3, bytes_accessed=rows * cols * 4, transcendentals=0
        ),
        name="kernel_update",
    )(where, xr, xc, xp, ihi, ilo)
    return (factor_rows, updated)


def solution(mesh):
    in_specs = (P(None, ("row", "col")), P(), P(("row", "col"), None), P(("row", "col")), P())
    out_specs = (P("row", None), P("row", "col"))

    def run(design_levels, length_scales, features, noise, panel_index):
        body = functools.partial(shards, design_levels.shape[1], 512)
        return jax.shard_map(
            body, mesh=mesh, in_specs=in_specs, out_specs=out_specs, check_vma=False
        )(design_levels, length_scales, features, noise, panel_index)

    return run
```

```python
import functools
import math

import jax
import jax.numpy as jnp
from jax import lax
from jax.experimental import pallas as pl
from jax.experimental.pallas import tpu as pltpu
from jax.sharding import PartitionSpec as P

BF = jnp.bfloat16
F32 = jnp.float32
LOG2E = math.log2(math.e)
BASE = 128
STRIP = 8
EXT = 40
EK = 256


def split2(x):
    hi = x.astype(BF)
    return hi, (x - hi.astype(F32)).astype(BF)


def split3(x):
    hi = x.astype(BF)
    rest = x - hi.astype(F32)
    mid = rest.astype(BF)
    return hi, mid, (rest - mid.astype(F32)).astype(BF)


def bdot(a, b):
    return jnp.dot(a, b, preferred_element_type=F32)


def dot3(a, b):
    (ah, al), (bh, bl) = a, b
    return bdot(ah, bh) + (bdot(ah, bl) + bdot(al, bh))


def fdot(a, b, dims):
    return lax.dot_general(
        a, b, (dims, ((), ())), precision=lax.Precision.HIGHEST, preferred_element_type=F32
    )


def exponent_operand(ext, inputs, left):
    width = ext.shape[1]
    root = math.sqrt(LOG2E)
    u = ext[:inputs] * root
    h, m, l = [part.astype(F32) for part in split3(u)]
    s = ext[inputs : inputs + 1] * (-0.5 * LOG2E)
    sh, sm, sl = [part.astype(F32) for part in split3(s)]
    row = lax.broadcasted_iota(jnp.int32, (8, width), 0)
    one = jnp.ones((8, width), F32)
    zero = jnp.zeros((8, width), F32)

    def norms(first):
        mine = jnp.where(
            row == first, sh, jnp.where(row == first + 1, sm, jnp.where(row == first + 2, sl, zero))
        )
        other = 3 - first
        ones = jnp.where((row >= other) & (row < other + 3), one, zero)
        return mine + ones

    if left:
        parts = [h, h, m, h, l, m, norms(0)]
    else:
        parts = [h, m, h, l, h, m, norms(3)]
    depth = 6 * inputs + 8
    parts.append(jnp.zeros((EK - depth, width), F32))
    return jnp.concatenate(parts, axis=0)


def factor_diagonal(d):
    n = d.shape[0]
    eye = (
        lax.broadcasted_iota(jnp.int32, (n, n), 0) == lax.broadcasted_iota(jnp.int32, (n, n), 1)
    ).astype(F32)
    rest_a = d
    rest_i = eye
    sub = lax.broadcasted_iota(jnp.int32, (STRIP, 1), 0)
    done = []
    for j in range(n // STRIP):
        strip = jnp.concatenate([rest_a[:STRIP], rest_i[:STRIP]], axis=1)
        first = j * STRIP
        cols = [
            jnp.broadcast_to(strip[:, first + i : first + i + 1], (STRIP, n)) for i in range(STRIP)
        ]
        for i in range(STRIP):
            inv = lax.rsqrt(cols[i][i : i + 1])
            col = cols[i] * inv
            row = strip[i : i + 1] * jnp.concatenate([inv, inv], axis=1)
            below = jnp.where(sub > i, col, 0.0)
            strip = jnp.where(sub == i, row, strip - jnp.concatenate([below, below], axis=1) * row)
            for k in range(i + 1, STRIP):
                cols[k] = cols[k] - below * col[k : k + 1]
        done.append(strip[:, n:])
        if j + 1 < n // STRIP:
            lead = strip[:, :n]
            change = fdot(lead, strip, ((0,), (0,)))[first + STRIP :]
            rest_a = rest_a[STRIP:] - change[:, :n]
            rest_i = rest_i[STRIP:] - change[:, n:]
    return jnp.concatenate(done, axis=0)


def inverse_kernel(inputs, feats, x_ref, hi_ref, lo_ref, t_ref):
    panel = x_ref.shape[1]
    h = x_ref[:feats, :]
    ext = x_ref[feats:, :]
    left = exponent_operand(ext, inputs, True).astype(BF)
    right = exponent_operand(ext, inputs, False).astype(BF)
    e = lax.dot_general(left, right, (((0,), (0,)), ((), ())), preferred_element_type=F32)
    gram = fdot(h, h, ((0,), (0,)))
    rows = lax.broadcasted_iota(jnp.int32, (panel, panel), 0)
    cols = lax.broadcasted_iota(jnp.int32, (panel, panel), 1)
    noise = ext[inputs + 1 : inputs + 2]
    t_ref[...] = jnp.exp2(e) + gram + jnp.where(rows == cols, noise, 0.0)
    count = panel // BASE
    for b in range(count):
        here = pl.ds(b * BASE, BASE)
        w = factor_diagonal(t_ref[here, here])
        r = fdot(w, t_ref[here, :], ((1,), (0,)))
        t_ref[here, :] = r
        t_ref[here, here] = w
        if b + 1 < count:
            below = pl.ds((b + 1) * BASE, panel - (b + 1) * BASE)
            t_ref[below, here] = jnp.zeros((panel - (b + 1) * BASE, BASE), F32)
            t_ref[below, :] = t_ref[below, :] - fdot(
                t_ref[here, below], t_ref[here, :], ((0,), (0,))
            )
    inverse = jnp.where(rows >= cols, t_ref[...], 0.0)
    hi, lo = split2(inverse)
    hi_ref[...] = hi
    lo_ref[...] = lo


def spread_kernel(bits, n_cols, bounds, x_ref, o_ref, buf, send, recv):
    me = lax.axis_index("row") * n_cols + lax.axis_index("col")
    partners = []
    for k in range(bits):
        bit = lax.rem(lax.div(me, 2**k), 2)
        other = me + 2**k * (1 - 2 * bit)
        partners.append((lax.div(other, n_cols), lax.rem(other, n_cols)))
    barrier = pltpu.get_barrier_semaphore()
    for device in partners:
        pl.semaphore_signal(
            barrier, inc=1, device_id=device, device_id_type=pl.DeviceIdType.MESH
        )
    pl.semaphore_wait(barrier, bits)
    o_ref[...] = x_ref[...]

    def copy(s, q):
        here = pl.ds(bounds[q], bounds[q + 1] - bounds[q])
        return pltpu.make_async_remote_copy(
            src_ref=o_ref.at[here],
            dst_ref=buf.at[s, here],
            send_sem=send.at[s, q],
            recv_sem=recv.at[s, q],
            device_id=partners[(s + q) % bits],
            device_id_type=pl.DeviceIdType.MESH,
        )

    chunks = len(bounds) - 1
    flying = [copy(0, q) for q in range(chunks)]
    for one in flying:
        one.start()
    for s in range(bits):
        for q in range(chunks):
            flying[q].wait()
            here = pl.ds(bounds[q], bounds[q + 1] - bounds[q])
            o_ref[here, :] = o_ref[here, :] + buf[s, here, :]
            if s + 1 < bits:
                flying[q] = copy(s + 1, q)
                flying[q].start()


def spread(part):
    n_rows = lax.axis_size("row")
    n_cols = lax.axis_size("col")
    bits = (n_rows * n_cols - 1).bit_length()
    depth, panel = part.shape
    groups = depth // 8
    bounds = [8 * (groups * q // bits) for q in range(bits + 1)]
    return pl.pallas_call(
        functools.partial(spread_kernel, bits, n_cols, bounds),
        out_shape=jax.ShapeDtypeStruct(part.shape, F32),
        in_specs=[pl.BlockSpec(memory_space=pltpu.VMEM)],
        out_specs=pl.BlockSpec(memory_space=pltpu.VMEM),
        scratch_shapes=[
            pltpu.VMEM((bits, depth, panel), F32),
            pltpu.SemaphoreType.DMA((bits, bits)),
            pltpu.SemaphoreType.DMA((bits, bits)),
        ],
        compiler_params=pltpu.CompilerParams(
            collective_id=0, has_side_effects=True, vmem_limit_bytes=16 * 2**20
        ),
        name="panel_spread",
    )(part)


def main_kernel(
    inputs,
    feats,
    n_row,
    n_col,
    bm,
    bn,
    where_ref,
    xr_ref,
    xc_ref,
    xp_ref,
    ihi_ref,
    ilo_ref,
    pf_ref,
    out_ref,
    ah,
    al,
    ea,
    bh,
    bl,
    eb,
    pt,
    ptl,
    pe,
    pel,
    ph,
    phl,
    it,
    itl,
    nr,
):
    step = pl.program_id(0)
    panel = xp_ref.shape[1]
    pts = xr_ref.shape[2]
    half = panel // 2
    row_start = where_ref[0]
    col_start = where_ref[1]
    panel_start = where_ref[2]

    @pl.when(step == 0)
    def _():
        hp = xp_ref[:feats, :]
        ext = xp_ref[feats:, :]
        hi, lo = split2(hp)
        ph[...] = hi
        phl[...] = lo
        hi, lo = split2(hp.T)
        pt[...] = hi
        ptl[...] = lo
        pe[...] = exponent_operand(ext, inputs, False).astype(BF)
        pel[...] = exponent_operand(ext, inputs, True).T.astype(BF)
        it[...] = ihi_ref[...].astype(F32).T.astype(BF)
        itl[...] = ilo_ref[...].astype(F32).T.astype(BF)

    @pl.when(step < n_row)
    def _():
        h = split2(xr_ref[0, :feats, :].T)
        ext = xr_ref[0, feats:, :]
        e = exponent_operand(ext, inputs, True).T.astype(BF)
        k = jnp.exp2(bdot(e, pe[...])) + dot3(h, (ph[...], phl[...]))
        first = row_start + step * pts
        rows = first + lax.broadcasted_iota(jnp.int32, (pts, panel), 0)
        cols = panel_start + lax.broadcasted_iota(jnp.int32, (pts, panel), 1)
        noise_col = ext[inputs : inputs + 8].T[:, 1:2]
        k = k + jnp.where(rows == cols, noise_col, 0.0)
        kh, kl = split2(k)
        p0 = dot3(
            (kh[:, :half], kl[:, :half]), (it[:half, :half], itl[:half, :half])
        )
        p1 = dot3((kh, kl), (it[:, half:], itl[:, half:]))
        p = jnp.concatenate([p0, p1], axis=1)
        pf_ref[...] = p
        phi, plo = split2(-p)
        here = pl.ds(pl.multiple_of(step * pts, pts), pts)
        ah[here, :feats] = h[0]
        al[here, :feats] = h[1]
        ah[here, feats:] = phi
        al[here, feats:] = plo
        ea[here, :] = e
        nr[here, :] = jnp.broadcast_to(noise_col, (pts, 128))

    @pl.when((step >= n_row) & (step < n_row + n_col))
    def _():
        at = step - n_row
        h = split2(xc_ref[0, :feats, :])
        ext = xc_ref[0, feats:, :]
        e = exponent_operand(ext, inputs, False).astype(BF)
        k = jnp.exp2(bdot(pel[...], e)) + dot3((pt[...], ptl[...]), h)
        first = col_start + at * pts
        rows = panel_start + lax.broadcasted_iota(jnp.int32, (panel, pts), 0)
        cols = first + lax.broadcasted_iota(jnp.int32, (panel, pts), 1)
        k = k + jnp.where(rows == cols, ext[inputs + 1 : inputs + 2], 0.0)
        kh, kl = split2(k)
        p0 = dot3(
            (ihi_ref[:half, :half], ilo_ref[:half, :half]), (kh[:half], kl[:half])
        )
        p1 = dot3((ihi_ref[half:, :], ilo_ref[half:, :]), (kh, kl))
        phi, plo = split2(jnp.concatenate([p0, p1], axis=0))
        here = pl.ds(pl.multiple_of(at * pts, pts), pts)
        bh[:feats, here] = h[0]
        bl[:feats, here] = h[1]
        bh[feats:, here] = phi
        bl[feats:, here] = plo
        eb[:, here] = e

    @pl.when(step >= n_row + n_col)
    def _():
        at = step - n_row - n_col
        per = eb.shape[1] // bn
        i = at // per
        j = at - i * per
        rs = pl.ds(pl.multiple_of(i * bm, bm), bm)
        cs = pl.ds(pl.multiple_of(j * bn, bn), bn)
        a = (ah[rs, :], al[rs, :])
        b = (bh[:, cs], bl[:, cs])
        out_ref[...] = jnp.exp2(bdot(ea[rs, :], eb[:, cs])) + dot3(a, b)
        r0 = row_start + i * bm
        c0 = col_start + j * bn

        @pl.when((r0 < c0 + bn) & (c0 < r0 + bm))
        def _():
            for q in range(bn // 128):
                rows = r0 + lax.broadcasted_iota(jnp.int32, (bm, 128), 0)
                cols = c0 + q * 128 + lax.broadcasted_iota(jnp.int32, (bm, 128), 1)
                part = pl.ds(q * 128, 128)
                out_ref[:, part] = out_ref[:, part] + jnp.where(rows == cols, nr[rs, :], 0.0)


def shards(n_total, panel, design_levels, length_scales, features, noise, panel_index):
    n_rows = lax.axis_size("row")
    n_cols = lax.axis_size("col")
    ratio = n_rows // n_cols
    row_pos = lax.axis_index("row")
    col_pos = lax.axis_index("col")
    inputs, pts = design_levels.shape
    feats = features.shape[1]
    depth = feats + EXT

    u = (design_levels.astype(F32) + 0.5) / n_total / length_scales[:, None]
    s = jnp.sum(u * u, axis=0, keepdims=True)
    pad = jnp.zeros((EXT - inputs - 2, pts), F32)
    piece = jnp.concatenate([features.T, u, s, noise[None, :], pad], axis=0)

    start = panel_index[0] * panel
    mine = (row_pos * n_cols + col_pos) * pts
    if pts == panel:
        part = jnp.where(mine == start, piece, 0.0)
    else:
        offset = mine - start
        inside = (offset >= 0) & (offset < panel)
        part = lax.dynamic_update_slice(
            jnp.zeros((depth, panel), F32),
            jnp.where(inside, piece, 0.0),
            (0, jnp.where(inside, offset, 0)),
        )
    xp = spread(part)

    xr = lax.all_gather(piece, "col", axis=0)
    pairs = []
    for r in range(n_rows):
        for c in range(n_cols):
            to = ((r % ratio) * n_cols + c) * n_cols + r // ratio
            pairs.append((r * n_cols + c, to))
    moved = lax.ppermute(piece, ("row", "col"), pairs)
    xc = lax.all_gather(moved, "row", axis=0)

    ihi, ilo = pl.pallas_call(
        functools.partial(inverse_kernel, inputs, feats),
        out_shape=[jax.ShapeDtypeStruct((panel, panel), BF)] * 2,
        in_specs=[pl.BlockSpec(memory_space=pltpu.VMEM)],
        out_specs=[pl.BlockSpec(memory_space=pltpu.VMEM)] * 2,
        scratch_shapes=[pltpu.VMEM((panel, panel), F32)],
        compiler_params=pltpu.CompilerParams(vmem_limit_bytes=40 * 2**20),
        cost_estimate=pl.CostEstimate(
            flops=60 * 10**9, bytes_accessed=2**21, transcendentals=2**18
        ),
        name="panel_inverse",
    )(xp)

    rows = pts * n_cols
    cols = pts * n_rows
    bm = min(512, rows)
    bn = min(1024, cols)
    per = cols // bn
    tiles = (rows // bm) * per
    lead = n_cols + n_rows
    row_start = row_pos * rows
    col_start = col_pos * cols
    where = jnp.stack([row_start, col_start, start]).astype(jnp.int32)

    def row_map(g, w):
        return (jnp.minimum(g, n_cols - 1), 0, 0)

    def col_map(g, w):
        return (jnp.clip(g - n_cols, 0, n_rows - 1), 0, 0)

    def out_map(g, w):
        t = jnp.maximum(g - lead, 0)
        return (t // per, t % per)

    k_all = feats + panel
    factor_rows, updated = pl.pallas_call(
        functools.partial(main_kernel, inputs, feats, n_cols, n_rows, bm, bn),
        out_shape=[
            jax.ShapeDtypeStruct((rows, panel), F32),
            jax.ShapeDtypeStruct((rows, cols), F32),
        ],
        grid_spec=pltpu.PrefetchScalarGridSpec(
            num_scalar_prefetch=1,
            grid=(lead + tiles,),
            in_specs=[
                pl.BlockSpec((1, depth, pts), row_map),
                pl.BlockSpec((1, depth, pts), col_map),
                pl.BlockSpec((depth, panel), lambda g, w: (0, 0)),
                pl.BlockSpec((panel, panel), lambda g, w: (0, 0)),
                pl.BlockSpec((panel, panel), lambda g, w: (0, 0)),
            ],
            out_specs=[
                pl.BlockSpec((pts, panel), lambda g, w: (jnp.minimum(g, n_cols - 1), 0)),
                pl.BlockSpec((bm, bn), out_map),
            ],
            scratch_shapes=[
                pltpu.VMEM((rows, k_all), BF),
                pltpu.VMEM((rows, k_all), BF),
                pltpu.VMEM((rows, EK), BF),
                pltpu.VMEM((k_all, cols), BF),
                pltpu.VMEM((k_all, cols), BF),
                pltpu.VMEM((EK, cols), BF),
                pltpu.VMEM((panel, feats), BF),
                pltpu.VMEM((panel, feats), BF),
                pltpu.VMEM((EK, panel), BF),
                pltpu.VMEM((panel, EK), BF),
                pltpu.VMEM((feats, panel), BF),
                pltpu.VMEM((feats, panel), BF),
                pltpu.VMEM((panel, panel), BF),
                pltpu.VMEM((panel, panel), BF),
                pltpu.VMEM((rows, 128), F32),
            ],
        ),
        compiler_params=pltpu.CompilerParams(
            dimension_semantics=("arbitrary",), vmem_limit_bytes=56 * 2**20
        ),
        cost_estimate=pl.CostEstimate(
            flops=2 * rows * cols * k_all * 3, bytes_accessed=rows * cols * 4, transcendentals=0
        ),
        name="kernel_update",
    )(where, xr, xc, xp, ihi, ilo)
    return (factor_rows, updated)


def solution(mesh):
    in_specs = (P(None, ("row", "col")), P(), P(("row", "col"), None), P(("row", "col")), P())
    out_specs = (P("row", None), P("row", "col"))

    def run(design_levels, length_scales, features, noise, panel_index):
        body = functools.partial(shards, design_levels.shape[1], 512)
        return jax.shard_map(
            body, mesh=mesh, in_specs=in_specs, out_specs=out_specs, check_vma=False
        )(design_levels, length_scales, features, noise, panel_index)

    return run
```

```python
import functools
import math

import jax
import jax.numpy as jnp
from jax import lax
from jax.experimental import pallas as pl
from jax.experimental.pallas import tpu as pltpu
from jax.sharding import PartitionSpec as P

BF = jnp.bfloat16
F32 = jnp.float32
LOG2E = math.log2(math.e)
BASE = 128
STRIP = 8
EXT = 40
EK = 256


def split2(x):
    hi = x.astype(BF)
    return hi, (x - hi.astype(F32)).astype(BF)


def split3(x):
    hi = x.astype(BF)
    rest = x - hi.astype(F32)
    mid = rest.astype(BF)
    return hi, mid, (rest - mid.astype(F32)).astype(BF)


def bdot(a, b):
    return jnp.dot(a, b, preferred_element_type=F32)


def dot3(a, b):
    (ah, al), (bh, bl) = a, b
    return bdot(ah, bh) + (bdot(ah, bl) + bdot(al, bh))


def fdot(a, b, dims):
    return lax.dot_general(
        a, b, (dims, ((), ())), precision=lax.Precision.HIGHEST, preferred_element_type=F32
    )


def exponent_operand(ext, inputs, left):
    width = ext.shape[1]
    root = math.sqrt(LOG2E)
    u = ext[:inputs] * root
    h, m, l = [part.astype(F32) for part in split3(u)]
    s = ext[inputs : inputs + 1] * (-0.5 * LOG2E)
    sh, sm, sl = [part.astype(F32) for part in split3(s)]
    row = lax.broadcasted_iota(jnp.int32, (8, width), 0)
    one = jnp.ones((8, width), F32)
    zero = jnp.zeros((8, width), F32)

    def norms(first):
        mine = jnp.where(
            row == first, sh, jnp.where(row == first + 1, sm, jnp.where(row == first + 2, sl, zero))
        )
        other = 3 - first
        ones = jnp.where((row >= other) & (row < other + 3), one, zero)
        return mine + ones

    if left:
        parts = [h, h, m, h, l, m, norms(0)]
    else:
        parts = [h, m, h, l, h, m, norms(3)]
    depth = 6 * inputs + 8
    parts.append(jnp.zeros((EK - depth, width), F32))
    return jnp.concatenate(parts, axis=0)


def factor_diagonal(d):
    n = d.shape[0]
    eye = (
        lax.broadcasted_iota(jnp.int32, (n, n), 0) == lax.broadcasted_iota(jnp.int32, (n, n), 1)
    ).astype(F32)
    rest_a = d
    rest_i = eye
    sub = lax.broadcasted_iota(jnp.int32, (STRIP, 1), 0)
    done = []
    for j in range(n // STRIP):
        strip = jnp.concatenate([rest_a[:STRIP], rest_i[:STRIP]], axis=1)
        first = j * STRIP
        cols = [
            jnp.broadcast_to(strip[:, first + i : first + i + 1], (STRIP, n)) for i in range(STRIP)
        ]
        for i in range(STRIP):
            inv = lax.rsqrt(cols[i][i : i + 1])
            col = cols[i] * inv
            row = strip[i : i + 1] * jnp.concatenate([inv, inv], axis=1)
            below = jnp.where(sub > i, col, 0.0)
            strip = jnp.where(sub == i, row, strip - jnp.concatenate([below, below], axis=1) * row)
            for k in range(i + 1, STRIP):
                cols[k] = cols[k] - below * col[k : k + 1]
        done.append(strip[:, n:])
        if j + 1 < n // STRIP:
            lead = strip[:, :n]
            change = fdot(lead, strip, ((0,), (0,)))[first + STRIP :]
            rest_a = rest_a[STRIP:] - change[:, :n]
            rest_i = rest_i[STRIP:] - change[:, n:]
    return jnp.concatenate(done, axis=0)


def inverse_kernel(inputs, feats, x_ref, hi_ref, lo_ref, t_ref):
    panel = x_ref.shape[1]
    h = x_ref[:feats, :]
    ext = x_ref[feats:, :]
    left = exponent_operand(ext, inputs, True).astype(BF)
    right = exponent_operand(ext, inputs, False).astype(BF)
    e = lax.dot_general(left, right, (((0,), (0,)), ((), ())), preferred_element_type=F32)
    gram = fdot(h, h, ((0,), (0,)))
    rows = lax.broadcasted_iota(jnp.int32, (panel, panel), 0)
    cols = lax.broadcasted_iota(jnp.int32, (panel, panel), 1)
    noise = ext[inputs + 1 : inputs + 2]
    t_ref[...] = jnp.exp2(e) + gram + jnp.where(rows == cols, noise, 0.0)
    count = panel // BASE
    for b in range(count):
        here = pl.ds(b * BASE, BASE)
        w = factor_diagonal(t_ref[here, here])
        r = fdot(w, t_ref[here, :], ((1,), (0,)))
        t_ref[here, :] = r
        t_ref[here, here] = w
        if b + 1 < count:
            below = pl.ds((b + 1) * BASE, panel - (b + 1) * BASE)
            t_ref[below, here] = jnp.zeros((panel - (b + 1) * BASE, BASE), F32)
            t_ref[below, :] = t_ref[below, :] - fdot(
                t_ref[here, below], t_ref[here, :], ((0,), (0,))
            )
    inverse = jnp.where(rows >= cols, t_ref[...], 0.0)
    hi, lo = split2(inverse)
    hi_ref[...] = hi
    lo_ref[...] = lo


def spread_kernel(bits, n_cols, bounds, x_ref, mine_ref, o_ref, all_ref, buf, send, recv, send_all, recv_all):
    col = lax.axis_index("col")
    me = lax.axis_index("row") * n_cols + col
    partners = []
    for k in range(bits):
        bit = lax.rem(lax.div(me, 2**k), 2)
        other = me + 2**k * (1 - 2 * bit)
        partners.append((lax.div(other, n_cols), lax.rem(other, n_cols)))
    barrier = pltpu.get_barrier_semaphore()
    for device in partners:
        pl.semaphore_signal(
            barrier, inc=1, device_id=device, device_id_type=pl.DeviceIdType.MESH
        )
    pl.semaphore_wait(barrier, bits)
    o_ref[...] = x_ref[...]
    all_ref[col] = mine_ref[...]
    col_bits = (n_cols - 1).bit_length()

    def row_copies(s):
        k = col_bits - 1 - s
        low = lax.rem(col, 2 ** (k + 1))
        return [
            pltpu.make_async_remote_copy(
                src_ref=all_ref.at[low + 2 ** (k + 1) * upper],
                dst_ref=all_ref.at[low + 2 ** (k + 1) * upper],
                send_sem=send_all.at[s, upper],
                recv_sem=recv_all.at[s, upper],
                device_id=partners[k],
                device_id_type=pl.DeviceIdType.MESH,
            )
            for upper in range(2**s)
        ]

    def copy(s, q):
        here = pl.ds(bounds[q], bounds[q + 1] - bounds[q])
        return pltpu.make_async_remote_copy(
            src_ref=o_ref.at[here],
            dst_ref=buf.at[s, here],
            send_sem=send.at[s, q],
            recv_sem=recv.at[s, q],
            device_id=partners[(s + q) % bits],
            device_id_type=pl.DeviceIdType.MESH,
        )

    chunks = len(bounds) - 1
    flying = [copy(0, q) for q in range(chunks)]
    for one in flying:
        one.start()
    row_flying = row_copies(0)
    for one in row_flying:
        one.start()
    for s in range(bits):
        for q in range(chunks):
            flying[q].wait()
            here = pl.ds(bounds[q], bounds[q + 1] - bounds[q])
            o_ref[here, :] = o_ref[here, :] + buf[s, here, :]
            if s + 1 < bits:
                flying[q] = copy(s + 1, q)
                flying[q].start()
        stage = s - (bits - 1 - col_bits)
        if stage >= 0:
            for one in row_flying:
                one.wait()
            row_flying = []
            if stage + 1 < col_bits:
                row_flying = row_copies(stage + 1)
                for one in row_flying:
                    one.start()


def spread(part, piece):
    n_rows = lax.axis_size("row")
    n_cols = lax.axis_size("col")
    bits = (n_rows * n_cols - 1).bit_length()
    depth, panel = part.shape
    groups = depth // 8
    bounds = [8 * (groups * q // bits) for q in range(bits + 1)]
    return pl.pallas_call(
        functools.partial(spread_kernel, bits, n_cols, bounds),
        out_shape=[
            jax.ShapeDtypeStruct(part.shape, F32),
            jax.ShapeDtypeStruct((n_cols,) + piece.shape, F32),
        ],
        in_specs=[pl.BlockSpec(memory_space=pltpu.VMEM)] * 2,
        out_specs=[pl.BlockSpec(memory_space=pltpu.VMEM)] * 2,
        scratch_shapes=[
            pltpu.VMEM((bits, depth, panel), F32),
            pltpu.SemaphoreType.DMA((bits, bits)),
            pltpu.SemaphoreType.DMA((bits, bits)),
            pltpu.SemaphoreType.DMA((bits, n_cols)),
            pltpu.SemaphoreType.DMA((bits, n_cols)),
        ],
        compiler_params=pltpu.CompilerParams(
            collective_id=0, has_side_effects=True, vmem_limit_bytes=16 * 2**20
        ),
        name="panel_spread",
    )(part, piece)


def main_kernel(
    inputs,
    feats,
    n_row,
    n_col,
    bm,
    bn,
    where_ref,
    xr_ref,
    xc_ref,
    xp_ref,
    ihi_ref,
    ilo_ref,
    pf_ref,
    out_ref,
    ah,
    al,
    ea,
    bh,
    bl,
    eb,
    pt,
    ptl,
    pe,
    pel,
    ph,
    phl,
    it,
    itl,
    nr,
):
    step = pl.program_id(0)
    panel = xp_ref.shape[1]
    pts = xr_ref.shape[2]
    half = panel // 2
    row_start = where_ref[0]
    col_start = where_ref[1]
    panel_start = where_ref[2]

    @pl.when(step == 0)
    def _():
        hp = xp_ref[:feats, :]
        ext = xp_ref[feats:, :]
        hi, lo = split2(hp)
        ph[...] = hi
        phl[...] = lo
        hi, lo = split2(hp.T)
        pt[...] = hi
        ptl[...] = lo
        pe[...] = exponent_operand(ext, inputs, False).astype(BF)
        pel[...] = exponent_operand(ext, inputs, True).T.astype(BF)
        it[...] = ihi_ref[...].astype(F32).T.astype(BF)
        itl[...] = ilo_ref[...].astype(F32).T.astype(BF)

    @pl.when(step < n_row)
    def _():
        h = split2(xr_ref[0, :feats, :].T)
        ext = xr_ref[0, feats:, :]
        e = exponent_operand(ext, inputs, True).T.astype(BF)
        k = jnp.exp2(bdot(e, pe[...])) + dot3(h, (ph[...], phl[...]))
        first = row_start + step * pts
        rows = first + lax.broadcasted_iota(jnp.int32, (pts, panel), 0)
        cols = panel_start + lax.broadcasted_iota(jnp.int32, (pts, panel), 1)
        noise_col = ext[inputs : inputs + 8].T[:, 1:2]
        k = k + jnp.where(rows == cols, noise_col, 0.0)
        kh, kl = split2(k)
        p0 = dot3(
            (kh[:, :half], kl[:, :half]), (it[:half, :half], itl[:half, :half])
        )
        p1 = dot3((kh, kl), (it[:, half:], itl[:, half:]))
        p = jnp.concatenate([p0, p1], axis=1)
        pf_ref[...] = p
        phi, plo = split2(-p)
        here = pl.ds(pl.multiple_of(step * pts, pts), pts)
        ah[here, :feats] = h[0]
        al[here, :feats] = h[1]
        ah[here, feats:] = phi
        al[here, feats:] = plo
        ea[here, :] = e
        nr[here, :] = jnp.broadcast_to(noise_col, (pts, 128))

    @pl.when((step >= n_row) & (step < n_row + n_col))
    def _():
        at = step - n_row
        h = split2(xc_ref[0, :feats, :])
        ext = xc_ref[0, feats:, :]
        e = exponent_operand(ext, inputs, False).astype(BF)
        k = jnp.exp2(bdot(pel[...], e)) + dot3((pt[...], ptl[...]), h)
        first = col_start + at * pts
        rows = panel_start + lax.broadcasted_iota(jnp.int32, (panel, pts), 0)
        cols = first + lax.broadcasted_iota(jnp.int32, (panel, pts), 1)
        k = k + jnp.where(rows == cols, ext[inputs + 1 : inputs + 2], 0.0)
        kh, kl = split2(k)
        p0 = dot3(
            (ihi_ref[:half, :half], ilo_ref[:half, :half]), (kh[:half], kl[:half])
        )
        p1 = dot3((ihi_ref[half:, :], ilo_ref[half:, :]), (kh, kl))
        phi, plo = split2(jnp.concatenate([p0, p1], axis=0))
        here = pl.ds(pl.multiple_of(at * pts, pts), pts)
        bh[:feats, here] = h[0]
        bl[:feats, here] = h[1]
        bh[feats:, here] = phi
        bl[feats:, here] = plo
        eb[:, here] = e

    @pl.when(step >= n_row + n_col)
    def _():
        at = step - n_row - n_col
        per = eb.shape[1] // bn
        i = at // per
        j = at - i * per
        rs = pl.ds(pl.multiple_of(i * bm, bm), bm)
        cs = pl.ds(pl.multiple_of(j * bn, bn), bn)
        a = (ah[rs, :], al[rs, :])
        b = (bh[:, cs], bl[:, cs])
        out_ref[...] = jnp.exp2(bdot(ea[rs, :], eb[:, cs])) + dot3(a, b)
        r0 = row_start + i * bm
        c0 = col_start + j * bn

        @pl.when((r0 < c0 + bn) & (c0 < r0 + bm))
        def _():
            for q in range(bn // 128):
                rows = r0 + lax.broadcasted_iota(jnp.int32, (bm, 128), 0)
                cols = c0 + q * 128 + lax.broadcasted_iota(jnp.int32, (bm, 128), 1)
                part = pl.ds(q * 128, 128)
                out_ref[:, part] = out_ref[:, part] + jnp.where(rows == cols, nr[rs, :], 0.0)


def shards(n_total, panel, design_levels, length_scales, features, noise, panel_index):
    n_rows = lax.axis_size("row")
    n_cols = lax.axis_size("col")
    ratio = n_rows // n_cols
    row_pos = lax.axis_index("row")
    col_pos = lax.axis_index("col")
    inputs, pts = design_levels.shape
    feats = features.shape[1]
    depth = feats + EXT

    u = (design_levels.astype(F32) + 0.5) / n_total / length_scales[:, None]
    s = jnp.sum(u * u, axis=0, keepdims=True)
    pad = jnp.zeros((EXT - inputs - 2, pts), F32)
    piece = jnp.concatenate([features.T, u, s, noise[None, :], pad], axis=0)

    start = panel_index[0] * panel
    mine = (row_pos * n_cols + col_pos) * pts
    if pts == panel:
        part = jnp.where(mine == start, piece, 0.0)
    else:
        offset = mine - start
        inside = (offset >= 0) & (offset < panel)
        part = lax.dynamic_update_slice(
            jnp.zeros((depth, panel), F32),
            jnp.where(inside, piece, 0.0),
            (0, jnp.where(inside, offset, 0)),
        )
    xp, xr = spread(part, piece)

    pairs = []
    for r in range(n_rows):
        for c in range(n_cols):
            to = ((r % ratio) * n_cols + c) * n_cols + r // ratio
            pairs.append((r * n_cols + c, to))
    moved = lax.ppermute(piece, ("row", "col"), pairs)
    xc = lax.all_gather(moved, "row", axis=0)

    ihi, ilo = pl.pallas_call(
        functools.partial(inverse_kernel, inputs, feats),
        out_shape=[jax.ShapeDtypeStruct((panel, panel), BF)] * 2,
        in_specs=[pl.BlockSpec(memory_space=pltpu.VMEM)],
        out_specs=[pl.BlockSpec(memory_space=pltpu.VMEM)] * 2,
        scratch_shapes=[pltpu.VMEM((panel, panel), F32)],
        compiler_params=pltpu.CompilerParams(vmem_limit_bytes=40 * 2**20),
        cost_estimate=pl.CostEstimate(
            flops=60 * 10**9, bytes_accessed=2**21, transcendentals=2**18
        ),
        name="panel_inverse",
    )(xp)

    rows = pts * n_cols
    cols = pts * n_rows
    bm = min(512, rows)
    bn = min(1024, cols)
    per = cols // bn
    tiles = (rows // bm) * per
    lead = n_cols + n_rows
    row_start = row_pos * rows
    col_start = col_pos * cols
    where = jnp.stack([row_start, col_start, start]).astype(jnp.int32)

    def row_map(g, w):
        return (jnp.minimum(g, n_cols - 1), 0, 0)

    def col_map(g, w):
        return (jnp.clip(g - n_cols, 0, n_rows - 1), 0, 0)

    def out_map(g, w):
        t = jnp.maximum(g - lead, 0)
        return (t // per, t % per)

    k_all = feats + panel
    factor_rows, updated = pl.pallas_call(
        functools.partial(main_kernel, inputs, feats, n_cols, n_rows, bm, bn),
        out_shape=[
            jax.ShapeDtypeStruct((rows, panel), F32),
            jax.ShapeDtypeStruct((rows, cols), F32),
        ],
        grid_spec=pltpu.PrefetchScalarGridSpec(
            num_scalar_prefetch=1,
            grid=(lead + tiles,),
            in_specs=[
                pl.BlockSpec((1, depth, pts), row_map),
                pl.BlockSpec((1, depth, pts), col_map),
                pl.BlockSpec((depth, panel), lambda g, w: (0, 0)),
                pl.BlockSpec((panel, panel), lambda g, w: (0, 0)),
                pl.BlockSpec((panel, panel), lambda g, w: (0, 0)),
            ],
            out_specs=[
                pl.BlockSpec((pts, panel), lambda g, w: (jnp.minimum(g, n_cols - 1), 0)),
                pl.BlockSpec((bm, bn), out_map),
            ],
            scratch_shapes=[
                pltpu.VMEM((rows, k_all), BF),
                pltpu.VMEM((rows, k_all), BF),
                pltpu.VMEM((rows, EK), BF),
                pltpu.VMEM((k_all, cols), BF),
                pltpu.VMEM((k_all, cols), BF),
                pltpu.VMEM((EK, cols), BF),
                pltpu.VMEM((panel, feats), BF),
                pltpu.VMEM((panel, feats), BF),
                pltpu.VMEM((EK, panel), BF),
                pltpu.VMEM((panel, EK), BF),
                pltpu.VMEM((feats, panel), BF),
                pltpu.VMEM((feats, panel), BF),
                pltpu.VMEM((panel, panel), BF),
                pltpu.VMEM((panel, panel), BF),
                pltpu.VMEM((rows, 128), F32),
            ],
        ),
        compiler_params=pltpu.CompilerParams(
            dimension_semantics=("arbitrary",), vmem_limit_bytes=56 * 2**20
        ),
        cost_estimate=pl.CostEstimate(
            flops=2 * rows * cols * k_all * 3, bytes_accessed=rows * cols * 4, transcendentals=0
        ),
        name="kernel_update",
    )(where, xr, xc, xp, ihi, ilo)
    return (factor_rows, updated)


def solution(mesh):
    in_specs = (P(None, ("row", "col")), P(), P(("row", "col"), None), P(("row", "col")), P())
    out_specs = (P("row", None), P("row", "col"))

    def run(design_levels, length_scales, features, noise, panel_index):
        body = functools.partial(shards, design_levels.shape[1], 512)
        return jax.shard_map(
            body, mesh=mesh, in_specs=in_specs, out_specs=out_specs, check_vma=False
        )(design_levels, length_scales, features, noise, panel_index)

    return run
```

```python
import functools
import math

import jax
import jax.numpy as jnp
from jax import lax
from jax.experimental import pallas as pl
from jax.experimental.pallas import tpu as pltpu
from jax.sharding import PartitionSpec as P

BF = jnp.bfloat16
F32 = jnp.float32
LOG2E = math.log2(math.e)
BASE = 128
STRIP = 8
EXT = 40
EK = 256


def split2(x):
    hi = x.astype(BF)
    return hi, (x - hi.astype(F32)).astype(BF)


def split3(x):
    hi = x.astype(BF)
    rest = x - hi.astype(F32)
    mid = rest.astype(BF)
    return hi, mid, (rest - mid.astype(F32)).astype(BF)


def bdot(a, b):
    return jnp.dot(a, b, preferred_element_type=F32)


def dot3(a, b):
    (ah, al), (bh, bl) = a, b
    return bdot(ah, bh) + (bdot(ah, bl) + bdot(al, bh))


def fdot(a, b, dims):
    return lax.dot_general(
        a, b, (dims, ((), ())), precision=lax.Precision.HIGHEST, preferred_element_type=F32
    )


def exponent_operand(ext, inputs, left):
    width = ext.shape[1]
    root = math.sqrt(LOG2E)
    u = ext[:inputs] * root
    h, m, l = [part.astype(F32) for part in split3(u)]
    s = ext[inputs : inputs + 1] * (-0.5 * LOG2E)
    sh, sm, sl = [part.astype(F32) for part in split3(s)]
    row = lax.broadcasted_iota(jnp.int32, (8, width), 0)
    one = jnp.ones((8, width), F32)
    zero = jnp.zeros((8, width), F32)

    def norms(first):
        mine = jnp.where(
            row == first, sh, jnp.where(row == first + 1, sm, jnp.where(row == first + 2, sl, zero))
        )
        other = 3 - first
        ones = jnp.where((row >= other) & (row < other + 3), one, zero)
        return mine + ones

    if left:
        parts = [h, h, m, h, l, m, norms(0)]
    else:
        parts = [h, m, h, l, h, m, norms(3)]
    depth = 6 * inputs + 8
    parts.append(jnp.zeros((EK - depth, width), F32))
    return jnp.concatenate(parts, axis=0)


def factor_diagonal(d):
    n = d.shape[0]
    eye = (
        lax.broadcasted_iota(jnp.int32, (n, n), 0) == lax.broadcasted_iota(jnp.int32, (n, n), 1)
    ).astype(F32)
    rest_a = d
    rest_i = eye
    sub = lax.broadcasted_iota(jnp.int32, (STRIP, 1), 0)
    done = []
    for j in range(n // STRIP):
        strip = jnp.concatenate([rest_a[:STRIP], rest_i[:STRIP]], axis=1)
        first = j * STRIP
        cols = [
            jnp.broadcast_to(strip[:, first + i : first + i + 1], (STRIP, n)) for i in range(STRIP)
        ]
        for i in range(STRIP):
            inv = lax.rsqrt(cols[i][i : i + 1])
            col = cols[i] * inv
            row = strip[i : i + 1] * jnp.concatenate([inv, inv], axis=1)
            below = jnp.where(sub > i, col, 0.0)
            strip = jnp.where(sub == i, row, strip - jnp.concatenate([below, below], axis=1) * row)
            for k in range(i + 1, STRIP):
                cols[k] = cols[k] - below * col[k : k + 1]
        done.append(strip[:, n:])
        if j + 1 < n // STRIP:
            lead = strip[:, :n]
            change = fdot(lead, strip, ((0,), (0,)))[first + STRIP :]
            rest_a = rest_a[STRIP:] - change[:, :n]
            rest_i = rest_i[STRIP:] - change[:, n:]
    return jnp.concatenate(done, axis=0)


def inverse_kernel(inputs, feats, x_ref, hi_ref, lo_ref, t_ref):
    panel = x_ref.shape[1]
    h = x_ref[:feats, :]
    ext = x_ref[feats:, :]
    left = exponent_operand(ext, inputs, True).astype(BF)
    right = exponent_operand(ext, inputs, False).astype(BF)
    e = lax.dot_general(left, right, (((0,), (0,)), ((), ())), preferred_element_type=F32)
    gram = fdot(h, h, ((0,), (0,)))
    rows = lax.broadcasted_iota(jnp.int32, (panel, panel), 0)
    cols = lax.broadcasted_iota(jnp.int32, (panel, panel), 1)
    noise = ext[inputs + 1 : inputs + 2]
    t_ref[...] = jnp.exp2(e) + gram + jnp.where(rows == cols, noise, 0.0)
    count = panel // BASE
    for b in range(count):
        here = pl.ds(b * BASE, BASE)
        w = factor_diagonal(t_ref[here, here])
        r = fdot(w, t_ref[here, :], ((1,), (0,)))
        t_ref[here, :] = r
        t_ref[here, here] = w
        if b + 1 < count:
            below = pl.ds((b + 1) * BASE, panel - (b + 1) * BASE)
            t_ref[below, here] = jnp.zeros((panel - (b + 1) * BASE, BASE), F32)
            t_ref[below, :] = t_ref[below, :] - fdot(
                t_ref[here, below], t_ref[here, :], ((0,), (0,))
            )
    inverse = jnp.where(rows >= cols, t_ref[...], 0.0)
    hi, lo = split2(inverse)
    hi_ref[...] = hi
    lo_ref[...] = lo


def spread_kernel(bits, n_cols, bounds, x_ref, mine_ref, o_ref, all_ref, buf, send, recv, send_all, recv_all):
    col = lax.axis_index("col")
    me = lax.axis_index("row") * n_cols + col
    partners = []
    for k in range(bits):
        bit = lax.rem(lax.div(me, 2**k), 2)
        other = me + 2**k * (1 - 2 * bit)
        partners.append((lax.div(other, n_cols), lax.rem(other, n_cols)))
    barrier = pltpu.get_barrier_semaphore()
    for device in partners:
        pl.semaphore_signal(
            barrier, inc=1, device_id=device, device_id_type=pl.DeviceIdType.MESH
        )
    pl.semaphore_wait(barrier, bits)
    o_ref[...] = x_ref[...]
    all_ref[col] = mine_ref[...]
    col_bits = (n_cols - 1).bit_length()

    def row_copies(s):
        k = col_bits - 1 - s
        low = lax.rem(col, 2 ** (k + 1))
        return [
            pltpu.make_async_remote_copy(
                src_ref=all_ref.at[low + 2 ** (k + 1) * upper],
                dst_ref=all_ref.at[low + 2 ** (k + 1) * upper],
                send_sem=send_all.at[s, upper],
                recv_sem=recv_all.at[s, upper],
                device_id=partners[k],
                device_id_type=pl.DeviceIdType.MESH,
            )
            for upper in range(2**s)
        ]

    def copy(s, q):
        here = pl.ds(bounds[q], bounds[q + 1] - bounds[q])
        return pltpu.make_async_remote_copy(
            src_ref=o_ref.at[here],
            dst_ref=buf.at[s, here],
            send_sem=send.at[s, q],
            recv_sem=recv.at[s, q],
            device_id=partners[(s + q) % bits],
            device_id_type=pl.DeviceIdType.MESH,
        )

    chunks = len(bounds) - 1
    flying = [copy(0, q) for q in range(chunks)]
    for one in flying:
        one.start()
    row_flying = row_copies(0)
    for one in row_flying:
        one.start()
    for s in range(bits):
        for q in range(chunks):
            flying[q].wait()
            here = pl.ds(bounds[q], bounds[q + 1] - bounds[q])
            o_ref[here, :] = o_ref[here, :] + buf[s, here, :]
            if s + 1 < bits:
                flying[q] = copy(s + 1, q)
                flying[q].start()
        stage = s - (bits - 1 - col_bits)
        if stage >= 0:
            for one in row_flying:
                one.wait()
            row_flying = []
            if stage + 1 < col_bits:
                row_flying = row_copies(stage + 1)
                for one in row_flying:
                    one.start()


def spread(part, piece):
    n_rows = lax.axis_size("row")
    n_cols = lax.axis_size("col")
    bits = (n_rows * n_cols - 1).bit_length()
    depth, panel = part.shape
    groups = depth // 8
    bounds = [8 * (groups * q // bits) for q in range(bits + 1)]
    return pl.pallas_call(
        functools.partial(spread_kernel, bits, n_cols, bounds),
        out_shape=[
            jax.ShapeDtypeStruct(part.shape, F32),
            jax.ShapeDtypeStruct((n_cols,) + piece.shape, F32),
        ],
        in_specs=[pl.BlockSpec(memory_space=pltpu.VMEM)] * 2,
        out_specs=[pl.BlockSpec(memory_space=pltpu.VMEM)] * 2,
        scratch_shapes=[
            pltpu.VMEM((bits, depth, panel), F32),
            pltpu.SemaphoreType.DMA((bits, bits)),
            pltpu.SemaphoreType.DMA((bits, bits)),
            pltpu.SemaphoreType.DMA((bits, n_cols)),
            pltpu.SemaphoreType.DMA((bits, n_cols)),
        ],
        compiler_params=pltpu.CompilerParams(
            collective_id=0, has_side_effects=True, vmem_limit_bytes=16 * 2**20
        ),
        cost_estimate=pl.CostEstimate(
            flops=60 * 10**9, bytes_accessed=2**22, transcendentals=0
        ),
        name="panel_spread",
    )(part, piece)


def main_kernel(
    inputs,
    feats,
    n_row,
    n_col,
    bm,
    bn,
    where_ref,
    xr_ref,
    xc_ref,
    xp_ref,
    ihi_ref,
    ilo_ref,
    pf_ref,
    out_ref,
    ah,
    al,
    ea,
    bh,
    bl,
    eb,
    pt,
    ptl,
    pe,
    pel,
    ph,
    phl,
    it,
    itl,
    nr,
):
    step = pl.program_id(0)
    panel = xp_ref.shape[1]
    pts = xr_ref.shape[2]
    half = panel // 2
    row_start = where_ref[0]
    col_start = where_ref[1]
    panel_start = where_ref[2]

    @pl.when(step == 0)
    def _():
        hp = xp_ref[:feats, :]
        ext = xp_ref[feats:, :]
        hi, lo = split2(hp)
        ph[...] = hi
        phl[...] = lo
        hi, lo = split2(hp.T)
        pt[...] = hi
        ptl[...] = lo
        pe[...] = exponent_operand(ext, inputs, False).astype(BF)
        pel[...] = exponent_operand(ext, inputs, True).T.astype(BF)
        it[...] = ihi_ref[...].astype(F32).T.astype(BF)
        itl[...] = ilo_ref[...].astype(F32).T.astype(BF)

    @pl.when(step < n_row)
    def _():
        h = split2(xr_ref[0, :feats, :].T)
        ext = xr_ref[0, feats:, :]
        e = exponent_operand(ext, inputs, True).T.astype(BF)
        k = jnp.exp2(bdot(e, pe[...])) + dot3(h, (ph[...], phl[...]))
        first = row_start + step * pts
        rows = first + lax.broadcasted_iota(jnp.int32, (pts, panel), 0)
        cols = panel_start + lax.broadcasted_iota(jnp.int32, (pts, panel), 1)
        noise_col = ext[inputs : inputs + 8].T[:, 1:2]
        k = k + jnp.where(rows == cols, noise_col, 0.0)
        kh, kl = split2(k)
        p0 = dot3(
            (kh[:, :half], kl[:, :half]), (it[:half, :half], itl[:half, :half])
        )
        p1 = dot3((kh, kl), (it[:, half:], itl[:, half:]))
        p = jnp.concatenate([p0, p1], axis=1)
        pf_ref[...] = p
        phi, plo = split2(-p)
        here = pl.ds(pl.multiple_of(step * pts, pts), pts)
        ah[here, :feats] = h[0]
        al[here, :feats] = h[1]
        ah[here, feats:] = phi
        al[here, feats:] = plo
        ea[here, :] = e
        nr[here, :] = jnp.broadcast_to(noise_col, (pts, 128))

    @pl.when((step >= n_row) & (step < n_row + n_col))
    def _():
        at = step - n_row
        h = split2(xc_ref[0, :feats, :])
        ext = xc_ref[0, feats:, :]
        e = exponent_operand(ext, inputs, False).astype(BF)
        k = jnp.exp2(bdot(pel[...], e)) + dot3((pt[...], ptl[...]), h)
        first = col_start + at * pts
        rows = panel_start + lax.broadcasted_iota(jnp.int32, (panel, pts), 0)
        cols = first + lax.broadcasted_iota(jnp.int32, (panel, pts), 1)
        k = k + jnp.where(rows == cols, ext[inputs + 1 : inputs + 2], 0.0)
        kh, kl = split2(k)
        p0 = dot3(
            (ihi_ref[:half, :half], ilo_ref[:half, :half]), (kh[:half], kl[:half])
        )
        p1 = dot3((ihi_ref[half:, :], ilo_ref[half:, :]), (kh, kl))
        phi, plo = split2(jnp.concatenate([p0, p1], axis=0))
        here = pl.ds(pl.multiple_of(at * pts, pts), pts)
        bh[:feats, here] = h[0]
        bl[:feats, here] = h[1]
        bh[feats:, here] = phi
        bl[feats:, here] = plo
        eb[:, here] = e

    @pl.when(step >= n_row + n_col)
    def _():
        at = step - n_row - n_col
        per = eb.shape[1] // bn
        i = at // per
        j = at - i * per
        rs = pl.ds(pl.multiple_of(i * bm, bm), bm)
        cs = pl.ds(pl.multiple_of(j * bn, bn), bn)
        a = (ah[rs, :], al[rs, :])
        b = (bh[:, cs], bl[:, cs])
        out_ref[...] = jnp.exp2(bdot(ea[rs, :], eb[:, cs])) + dot3(a, b)
        r0 = row_start + i * bm
        c0 = col_start + j * bn

        @pl.when((r0 < c0 + bn) & (c0 < r0 + bm))
        def _():
            for q in range(bn // 128):
                rows = r0 + lax.broadcasted_iota(jnp.int32, (bm, 128), 0)
                cols = c0 + q * 128 + lax.broadcasted_iota(jnp.int32, (bm, 128), 1)
                part = pl.ds(q * 128, 128)
                out_ref[:, part] = out_ref[:, part] + jnp.where(rows == cols, nr[rs, :], 0.0)


def shards(n_total, panel, design_levels, length_scales, features, noise, panel_index):
    n_rows = lax.axis_size("row")
    n_cols = lax.axis_size("col")
    ratio = n_rows // n_cols
    row_pos = lax.axis_index("row")
    col_pos = lax.axis_index("col")
    inputs, pts = design_levels.shape
    feats = features.shape[1]
    depth = feats + EXT

    u = (design_levels.astype(F32) + 0.5) / n_total / length_scales[:, None]
    s = jnp.sum(u * u, axis=0, keepdims=True)
    pad = jnp.zeros((EXT - inputs - 2, pts), F32)
    piece = jnp.concatenate([features.T, u, s, noise[None, :], pad], axis=0)

    start = panel_index[0] * panel
    mine = (row_pos * n_cols + col_pos) * pts
    if pts == panel:
        part = jnp.where(mine == start, piece, 0.0)
    else:
        offset = mine - start
        inside = (offset >= 0) & (offset < panel)
        part = lax.dynamic_update_slice(
            jnp.zeros((depth, panel), F32),
            jnp.where(inside, piece, 0.0),
            (0, jnp.where(inside, offset, 0)),
        )
    xp, xr = spread(part, piece)

    pairs = []
    for r in range(n_rows):
        for c in range(n_cols):
            to = ((r % ratio) * n_cols + c) * n_cols + r // ratio
            pairs.append((r * n_cols + c, to))
    moved = lax.ppermute(piece, ("row", "col"), pairs)
    moved, xp = lax.optimization_barrier((moved, xp))
    xc = lax.all_gather(moved, "row", axis=0)

    ihi, ilo = pl.pallas_call(
        functools.partial(inverse_kernel, inputs, feats),
        out_shape=[jax.ShapeDtypeStruct((panel, panel), BF)] * 2,
        in_specs=[pl.BlockSpec(memory_space=pltpu.VMEM)],
        out_specs=[pl.BlockSpec(memory_space=pltpu.VMEM)] * 2,
        scratch_shapes=[pltpu.VMEM((panel, panel), F32)],
        compiler_params=pltpu.CompilerParams(vmem_limit_bytes=40 * 2**20),
        cost_estimate=pl.CostEstimate(
            flops=60 * 10**9, bytes_accessed=2**21, transcendentals=2**18
        ),
        name="panel_inverse",
    )(xp)

    rows = pts * n_cols
    cols = pts * n_rows
    bm = min(512, rows)
    bn = min(1024, cols)
    per = cols // bn
    tiles = (rows // bm) * per
    lead = n_cols + n_rows
    row_start = row_pos * rows
    col_start = col_pos * cols
    where = jnp.stack([row_start, col_start, start]).astype(jnp.int32)

    def row_map(g, w):
        return (jnp.minimum(g, n_cols - 1), 0, 0)

    def col_map(g, w):
        return (jnp.clip(g - n_cols, 0, n_rows - 1), 0, 0)

    def out_map(g, w):
        t = jnp.maximum(g - lead, 0)
        return (t // per, t % per)

    k_all = feats + panel
    factor_rows, updated = pl.pallas_call(
        functools.partial(main_kernel, inputs, feats, n_cols, n_rows, bm, bn),
        out_shape=[
            jax.ShapeDtypeStruct((rows, panel), F32),
            jax.ShapeDtypeStruct((rows, cols), F32),
        ],
        grid_spec=pltpu.PrefetchScalarGridSpec(
            num_scalar_prefetch=1,
            grid=(lead + tiles,),
            in_specs=[
                pl.BlockSpec((1, depth, pts), row_map),
                pl.BlockSpec((1, depth, pts), col_map),
                pl.BlockSpec((depth, panel), lambda g, w: (0, 0)),
                pl.BlockSpec((panel, panel), lambda g, w: (0, 0)),
                pl.BlockSpec((panel, panel), lambda g, w: (0, 0)),
            ],
            out_specs=[
                pl.BlockSpec((pts, panel), lambda g, w: (jnp.minimum(g, n_cols - 1), 0)),
                pl.BlockSpec((bm, bn), out_map),
            ],
            scratch_shapes=[
                pltpu.VMEM((rows, k_all), BF),
                pltpu.VMEM((rows, k_all), BF),
                pltpu.VMEM((rows, EK), BF),
                pltpu.VMEM((k_all, cols), BF),
                pltpu.VMEM((k_all, cols), BF),
                pltpu.VMEM((EK, cols), BF),
                pltpu.VMEM((panel, feats), BF),
                pltpu.VMEM((panel, feats), BF),
                pltpu.VMEM((EK, panel), BF),
                pltpu.VMEM((panel, EK), BF),
                pltpu.VMEM((feats, panel), BF),
                pltpu.VMEM((feats, panel), BF),
                pltpu.VMEM((panel, panel), BF),
                pltpu.VMEM((panel, panel), BF),
                pltpu.VMEM((rows, 128), F32),
            ],
        ),
        compiler_params=pltpu.CompilerParams(
            dimension_semantics=("arbitrary",), vmem_limit_bytes=56 * 2**20
        ),
        cost_estimate=pl.CostEstimate(
            flops=2 * rows * cols * k_all * 3, bytes_accessed=rows * cols * 4, transcendentals=0
        ),
        name="kernel_update",
    )(where, xr, xc, xp, ihi, ilo)
    return (factor_rows, updated)


def solution(mesh):
    in_specs = (P(None, ("row", "col")), P(), P(("row", "col"), None), P(("row", "col")), P())
    out_specs = (P("row", None), P("row", "col"))

    def run(design_levels, length_scales, features, noise, panel_index):
        body = functools.partial(shards, design_levels.shape[1], 512)
        return jax.shard_map(
            body, mesh=mesh, in_specs=in_specs, out_specs=out_specs, check_vma=False
        )(design_levels, length_scales, features, noise, panel_index)

    return run
```
